32 devices in a mesh: dp: 4 (over z), tensor: 8 (over y, x, core).
Axes of the slice: x: 2, y: 2, z: 4, core: 2. Of those that a mesh axis runs over, the one named last changes fastest.
Arguments:
- tokens: bfloat16 [4, 1536, 4096], P('dp', 'tensor'), may hold values from -6 to 6
- ln_gain: float32 [4096], replicated, may hold values from 0.1 to 1.9
- ln_bias: float32 [4096], replicated, may hold values from -3 to 3
- w_qkv: bfloat16 [4096, 3, 4096], P(None, None, 'tensor'), may hold values from -0.375 to 0.375
- w_out: bfloat16 [4096, 4096], P(None, 'tensor'), may hold values from -0.09375 to 0.09375
- layer_scale: float32 [4096], P('tensor'), may hold values from 0.5 to 4
- w_merge: bfloat16 [4, 4096, 4096], P(None, 'tensor'), may hold values from -0.046875 to 0.046875
- segment_ids: int32 [4, 1536], P('dp'), may hold values from 0 to 3, as said below
- grid_sizes: int32 [4, 3, 2], P('dp'), may hold values from 14 to 28, as said below
- owners: int32 [4, 384, 1], P('dp'), may hold values from 0 to 31; in each aligned block of 384 rows (0 to 383, 384 to 767, ..., all dimensions but the last counted through in order) at most 18 rows name the same one
Outputs:
- received: bfloat16 [4, 576, 4096], P('dp', 'tensor')
The draws below stay inside these ranges and needn't reach their ends.
Inputs may be any that keep to these rules, and one draw needn't show every extreme that they name: `grid_sizes`: both sides of every grid are even; in every batch one image has sides 28 x 28 and the others have sides of at most 18. `segment_ids`: the images of a batch lie end to end from slot 0 in order; the 5 + h w slots of image i hold i, and the padding after the last image holds 3. `owners`: within one batch no owner is named by more than 18 rows, a bound that some block reaches.
All inputs are finite; a program needn't handle non-finite values.
Results may differ from the reference program's by a relative error of at most 0.01.
Values may be sent and summed in bfloat16 or wider, within the bound.
A program may use at most 128 MiB of HBM per device.

```python
import math
import jax
import jax.numpy as jnp
import numpy as np
from jax import lax

D = 4096
HEADS = 32
HEAD_DIM = 128
D_OUT = 4096
SEQ = 1536
IMGS = 3
REG = 5
GRID_MIN = 14
GRID_MAX = 28
BATCHES = 4
MERGED = 384
OWN_CAP = 18
N_DP = 4
N_TENSOR = 8
DEVICES = 32


def image_grids(key):
    folded = jax.random.fold_in(key, 11)
    big_key, side_key = jax.random.split(folded)
    big_index = jax.random.randint(big_key, (BATCHES,), 0, IMGS)
    half_sides = jax.random.randint(side_key, (BATCHES, IMGS, 2), GRID_MIN // 2, (GRID_MIN + 4) // 2 + 1)
    is_big = (jnp.arange(IMGS)[None, :] == big_index[:, None])[:, :, None]
    return jnp.where(is_big, GRID_MAX, 2 * half_sides).astype(jnp.int32)


def draw_grid_sizes(key, part):
    return image_grids(key)


def draw_segment_ids(key, part):
    grids = image_grids(key)
    lengths = REG + grids[:, :, 0] * grids[:, :, 1]
    ends = jnp.cumsum(lengths, axis=1)
    position = jnp.arange(SEQ, dtype=jnp.int32)
    return jnp.sum((position[None, :, None] >= ends[:, None, :]).astype(jnp.int32), axis=2).astype(jnp.int32)


def draw_w_qkv(key, part):
    folded = jax.random.fold_in(key, 23)
    base_key = jax.random.fold_in(folded, 0)
    base = jax.random.truncated_normal(base_key, -4.0, 4.0, (D, 3, D), jnp.float32) * D ** (-0.5)
    return base.astype(jnp.bfloat16)


def steps_of(key, dims, pieces, smallest, largest):
    gain = 1.0
    for dim, parts in pieces:
        steps = jax.random.uniform(jax.random.fold_in(jax.random.fold_in(key, 6), dim), (parts,), jnp.float32, smallest / len(pieces), largest / len(pieces))
        gain = gain * jnp.repeat(jnp.exp(steps), dims[dim] // parts).reshape((-1,) + (1,) * (len(dims) - 1 - dim))
    return gain


def routed_block(rng, own, number, rows, number_of, top, bound, skew):
    order = jax.random.permutation(rng, number_of)
    packed, ordinary = load_shares(number_of, rows * top, bound, skew, True), load_shares(number_of, rows * top, bound, skew, False)
    places = jnp.arange(number_of)

    def named(sizes, rotation):
        used = int((sizes > 0).sum())
        fixed = max(1, used // 4)
        passed = fixed + (places - fixed + rotation * (used - fixed)) % max(1, number_of - fixed)
        return jnp.zeros((number_of,), jnp.int32).at[order[jnp.where(places < fixed, places, passed)]].set(jnp.asarray(sizes, jnp.int32))

    sizes = jnp.where(number % 4 == 0, named(packed, number // 4), named(ordinary, number - number // 4 - 1))
    mixed = jax.random.permutation(jax.random.fold_in(own, 3), number_of)
    donor, taker = mixed[0:number_of // 2 * 2:2], mixed[1:number_of // 2 * 2:2]
    slack = jnp.minimum(sizes[donor] - 1, bound - sizes[taker]) // 2
    slack = jnp.where((donor == order[0]) | (taker == order[0]) | (sizes[taker] == 0), 0, jnp.maximum(slack, 0))
    passed = jax.random.randint(jax.random.fold_in(own, 4), (number_of // 2,), 0, 1 << 20) % (slack + 1)
    sizes = sizes.at[donor].add(-passed).at[taker].add(passed)
    members = jnp.searchsorted(jnp.cumsum(sizes), jnp.arange(rows * top), side="right").astype(jnp.int32)
    listing = members.reshape(top, rows).T
    listing = listing[jax.random.permutation(jax.random.fold_in(own, 1), rows)]
    rotation = jax.random.randint(jax.random.fold_in(own, 2), (rows, 1), 0, top)
    return jnp.take_along_axis(listing, (jnp.arange(top)[None, :] + rotation) % top, axis=1)


def load_shares(number_of, total, most, slope, full):
    loads = [(1 << 20) // math.isqrt(rank ** slope) + 1 for rank in range(1, number_of + 1)]
    largest = most if full else min(most, max(-(-total // number_of), total * loads[0] // sum(loads)))
    least = 1 if total - largest >= number_of - 1 else 0
    given, rest = [largest] + [least] * (number_of - 1), total - largest - least * (number_of - 1)
    while rest > 0:
        candidates = [i for i in range(1, number_of) if given[i] < largest] or [i for i in range(1, number_of) if given[i] < most]
        whole, remaining = sum([loads[i] for i in candidates]), rest
        for i in candidates:
            extra = min(most - given[i], max(1, remaining * loads[i] // whole), rest)
            given[i] = given[i] + extra
            rest = rest - extra
    return np.array(given)


def normal_values(own_key, shape, scale, reach, cuts=(), held_as=jnp.bfloat16):
    factor_of = steps_of(own_key, shape, cuts, -0.22, 0.18) if cuts else 1.0
    values = jax.random.normal(own_key, shape, jnp.float32) * scale * factor_of
    return jnp.minimum(jnp.maximum(values, -reach), reach).astype(held_as)


def setup_inputs(seed: int = 0) -> dict:
    key_of = jax.random.split(jax.random.key(seed), 11)
    tokens = normal_values(key_of[0], (BATCHES, SEQ, D), 1.0, 6.0, ((0, 4), (1, 8)))
    ln_gain = jnp.clip(1.0 + 0.18 * jax.random.normal(key_of[1], (D,), jnp.float32), 0.1, 1.9)
    ln_bias = normal_values(key_of[2], (D,), 0.5, 3.0, (), jnp.float32)
    w_qkv = draw_w_qkv(jax.random.fold_in(key_of[10], 71), 0)
    w_out = normal_values(key_of[4], (D, D), D ** -0.5, 0.09375, ((1, 8),))
    layer_scale = jnp.clip(jnp.exp(math.log(4.0) - 2.0794415 * jax.random.uniform(key_of[5], (D,), jnp.float32) ** steps_of(key_of[5], (D,), ((0, 8),), -0.2, 0.2)), 0.5, 4.0)
    w_merge = normal_values(key_of[6], (4, D, D_OUT), (4 * D) ** -0.5, 0.046875, ((1, 8),))
    segment_ids = draw_segment_ids(jax.random.fold_in(key_of[10], 71), 0)
    grid_sizes = draw_grid_sizes(jax.random.fold_in(key_of[10], 71), 0)
    owners_keys = jax.random.split(jax.random.fold_in(key_of[9], 1), BATCHES * MERGED // MERGED)
    owners_turns = jax.random.permutation(jax.random.fold_in(key_of[9], 3), BATCHES * MERGED // MERGED)
    owners = jax.vmap(lambda own, number: routed_block(jax.random.fold_in(key_of[9], 2), own, number, MERGED, DEVICES, 1, OWN_CAP, 2))(owners_keys, owners_turns).reshape((BATCHES, MERGED, 1))
    return {"tokens": tokens, "ln_gain": ln_gain, "ln_bias": ln_bias, "w_qkv": w_qkv, "w_out": w_out, "layer_scale": layer_scale, "w_merge": w_merge, "segment_ids": segment_ids, "grid_sizes": grid_sizes, "owners": owners}


norm_eps = 1e-06

def layer_norm(row_data, gain_vec, shift_vec):
    values = row_data.astype(jnp.float32)
    center = values - lax.optimization_barrier(jnp.mean(values, axis=-1, keepdims=True))
    spread = lax.optimization_barrier(jnp.mean(center * center, axis=-1, keepdims=True))
    return (center * lax.rsqrt(spread + norm_eps) * gain_vec + shift_vec).astype(jnp.bfloat16)

def image_layout(grid_row):
    heights = grid_row[:, 0]
    widths = grid_row[:, 1]
    lengths = REG + heights * widths
    starts = jnp.cumsum(lengths) - lengths
    counts = heights // 2 * (widths // 2)
    merged_end = jnp.cumsum(counts)
    return (heights, widths, starts, merged_end - counts, merged_end)

def pick_rows(onehot, lookup):
    return lax.optimization_barrier(jnp.sum(onehot * lookup[None, :], axis=1))

def rope_tables(seg_row, grid_row, seq_len):
    heights, widths, starts, first_merged, last_merged = image_layout(grid_row)
    position = jnp.arange(seq_len, dtype=jnp.int32)
    image_ids = jnp.arange(IMGS, dtype=jnp.int32)
    onehot = (seg_row[:, None] == image_ids[None, :]).astype(jnp.int32)
    is_image = lax.optimization_barrier(jnp.sum(onehot, axis=1)) > 0
    in_image = position - pick_rows(onehot, starts) - REG
    is_patch = is_image & (in_image >= 0)
    row_width = jnp.maximum(pick_rows(onehot, widths), 1)
    col_height = jnp.maximum(pick_rows(onehot, heights), 1)
    clipped = jnp.maximum(in_image, 0)
    coord_y = 2.0 * ((clipped // row_width).astype(jnp.float32) + 0.5) / col_height.astype(jnp.float32) - 1.0
    coord_x = 2.0 * ((clipped % row_width).astype(jnp.float32) + 0.5) / row_width.astype(jnp.float32) - 1.0
    quarter = HEAD_DIM // 4
    pair_ids = jnp.arange(HEAD_DIM // 2, dtype=jnp.int32)
    omegas = 100.0 ** ((pair_ids % quarter).astype(jnp.float32) / quarter)
    coord_all = jnp.where(pair_ids[None, :] < quarter, coord_y[:, None], coord_x[:, None])
    angles = jnp.where(is_patch[:, None], jnp.pi * omegas[None, :] * coord_all, 0.0)
    return (jnp.cos(angles), jnp.sin(angles))

def rotate(values, cos_rows, sin_rows):
    half_dim = values.shape[-1] // 2
    first_half = values[..., :half_dim]
    second_half = values[..., half_dim:]
    return jnp.concatenate([first_half * cos_rows - second_half * sin_rows, second_half * cos_rows + first_half * sin_rows], axis=-1)

def merge_sources(grid_row, merged_rows):
    heights, widths, starts, first_merged, last_merged = image_layout(grid_row)
    row_ids = jnp.arange(merged_rows, dtype=jnp.int32)
    onehot = ((row_ids[:, None] >= first_merged[None, :]) & (row_ids[:, None] < last_merged[None, :])).astype(jnp.int32)
    is_valid = lax.optimization_barrier(jnp.sum(onehot, axis=1)) > 0
    row_width = pick_rows(onehot, widths)
    half_width = jnp.maximum(row_width // 2, 1)
    in_image = row_ids - pick_rows(onehot, first_merged)
    corner = pick_rows(onehot, starts) + REG + 2 * (in_image // half_width) * row_width + 2 * (in_image % half_width)
    offsets = jnp.stack([jnp.zeros_like(row_width), jnp.ones_like(row_width), row_width, row_width + 1], axis=1)
    sources = jnp.where(is_valid[:, None], corner[:, None] + offsets, 0)
    return (sources.astype(jnp.int32), is_valid)

def attend(query_rows, query_seg, key_rows, value_rows, key_seg):
    scores = lax.dot_general(query_rows, key_rows, (((1,), (1,)), ((), ())), preferred_element_type=jnp.float32) * HEAD_DIM ** (-0.5)
    scores = jnp.where(query_seg[:, None] == key_seg[None, :], scores, -jnp.inf)
    shifted = jnp.exp(scores - lax.optimization_barrier(jnp.max(scores, axis=1, keepdims=True)))
    weights = (shifted / lax.optimization_barrier(jnp.sum(shifted, axis=1, keepdims=True))).astype(jnp.bfloat16)
    return jnp.dot(weights, value_rows, preferred_element_type=jnp.float32).astype(jnp.bfloat16)

def owner_ranks(owner_row, device_count):
    onehot = (owner_row[:, None] == jnp.arange(device_count, dtype=jnp.int32)[None, :]).astype(jnp.int32)
    before = jnp.cumsum(onehot, axis=0) - onehot
    return lax.optimization_barrier(jnp.sum(before * onehot, axis=1))

def batch_forward(x_rows, seg_row, grid_row, ln_gain, ln_bias, w_qkv, w_out, layer_scale, w_merge):
    seq_len = x_rows.shape[0]
    normed = layer_norm(x_rows, ln_gain, ln_bias)
    qkv_rows = jnp.dot(normed, w_qkv.reshape(D, 3 * D), preferred_element_type=jnp.float32)
    cos_table, sin_table = rope_tables(seg_row, grid_row, seq_len)
    cos_rows = cos_table[:, None, :]
    sin_rows = sin_table[:, None, :]
    query_all = rotate(qkv_rows[:, :D].reshape(seq_len, HEADS, HEAD_DIM), cos_rows, sin_rows).astype(jnp.bfloat16)
    key_all = rotate(qkv_rows[:, D:2 * D].reshape(seq_len, HEADS, HEAD_DIM), cos_rows, sin_rows).astype(jnp.bfloat16)
    value_all = qkv_rows[:, 2 * D:].reshape(seq_len, HEADS, HEAD_DIM).astype(jnp.bfloat16)

    def per_head(inputs):
        return attend(inputs[0], seg_row, inputs[1], inputs[2], seg_row)
    per_heads = lax.map(per_head, (query_all.transpose(1, 0, 2), key_all.transpose(1, 0, 2), value_all.transpose(1, 0, 2)))
    context = per_heads.transpose(1, 0, 2).reshape(seq_len, D)
    mixed = jnp.dot(context, w_out, preferred_element_type=jnp.float32)
    hidden = (x_rows.astype(jnp.float32) + layer_scale * mixed).astype(jnp.bfloat16)
    merged_rows = seq_len // 4
    sources, is_valid = merge_sources(grid_row, merged_rows)
    merged = jnp.where(is_valid[:, None, None], hidden[sources], jnp.zeros((), jnp.bfloat16))
    col_width = D // N_TENSOR

    def add_group(running, group_index):
        offset = (group_index * col_width).astype(jnp.int32)
        columns = lax.dynamic_slice_in_dim(merged, offset, col_width, 2).reshape(merged_rows, 4 * col_width)
        weight_rows = lax.dynamic_slice_in_dim(w_merge, offset, col_width, 1).reshape(4 * col_width, D_OUT)
        term_part = jnp.dot(columns, weight_rows, preferred_element_type=jnp.float32)
        return (running + lax.optimization_barrier(term_part.astype(jnp.bfloat16)).astype(jnp.float32), None)
    total, unused = lax.scan(add_group, jnp.zeros((merged_rows, D_OUT), jnp.float32), jnp.arange(N_TENSOR, dtype=jnp.int32))
    return total.astype(jnp.bfloat16)

def reference(tokens, ln_gain, ln_bias, w_qkv, w_out, layer_scale, w_merge, segment_ids, grid_sizes, owners):
    outputs = []
    slot_lists = []
    for batch_index in range(BATCHES):
        outputs.append(batch_forward(tokens[batch_index], segment_ids[batch_index], grid_sizes[batch_index], ln_gain, ln_bias, w_qkv, w_out, layer_scale, w_merge))
        owner_row = owners[batch_index, :, 0]
        ranks = owner_ranks(owner_row, DEVICES)
        slot_lists.append(owner_row * (N_DP * OWN_CAP) + batch_index * OWN_CAP + ranks)
    rows_all = jnp.concatenate(outputs, axis=0)
    slots = jnp.concatenate(slot_lists, axis=0).astype(jnp.int32)
    placed = jnp.zeros((DEVICES * N_DP * OWN_CAP, D_OUT), jnp.bfloat16).at[slots].set(rows_all)
    return placed.reshape(BATCHES, N_TENSOR * N_DP * OWN_CAP, D_OUT)
```

```python
import jax
import jax.numpy as jnp
from jax import lax
from jax.experimental import pallas as pl
from jax.experimental.pallas import tpu as pltpu
from jax.sharding import PartitionSpec as P

HEAD_DIM = 128
IMGS = 3
REG = 5


norm_eps = 1e-06


def layer_norm(row_data, gain_vec, shift_vec):
    values = row_data.astype(jnp.float32)
    center = values - jnp.mean(values, axis=-1, keepdims=True)
    spread = jnp.mean(center * center, axis=-1, keepdims=True)
    return (center * lax.rsqrt(spread + norm_eps) * gain_vec + shift_vec).astype(jnp.bfloat16)


def running_sum(values):
    count = values.shape[0]
    lower = jnp.arange(count)[:, None] >= jnp.arange(count)[None, :]
    return jnp.sum(jnp.where(lower, values[None, :], 0), axis=1)


def image_layout(grid_row):
    heights = grid_row[:, 0]
    widths = grid_row[:, 1]
    lengths = REG + heights * widths
    starts = running_sum(lengths) - lengths
    counts = heights // 2 * (widths // 2)
    merged_end = running_sum(counts)
    return (heights, widths, starts, merged_end - counts, merged_end)


def pick_rows(onehot, lookup):
    return jnp.sum(onehot * lookup[None, :], axis=1)


def rope_tables(seg_row, grid_row, seq_len):
    heights, widths, starts, first_merged, last_merged = image_layout(grid_row)
    position = jnp.arange(seq_len, dtype=jnp.int32)
    image_ids = jnp.arange(IMGS, dtype=jnp.int32)
    onehot = (seg_row[:, None] == image_ids[None, :]).astype(jnp.int32)
    is_image = jnp.sum(onehot, axis=1) > 0
    in_image = position - pick_rows(onehot, starts) - REG
    is_patch = is_image & (in_image >= 0)
    row_width = jnp.maximum(pick_rows(onehot, widths), 1)
    col_height = jnp.maximum(pick_rows(onehot, heights), 1)
    clipped = jnp.maximum(in_image, 0)
    coord_y = (
        2.0 * ((clipped // row_width).astype(jnp.float32) + 0.5) / col_height.astype(jnp.float32)
        - 1.0
    )
    coord_x = (
        2.0 * ((clipped % row_width).astype(jnp.float32) + 0.5) / row_width.astype(jnp.float32)
        - 1.0
    )
    quarter = HEAD_DIM // 4
    pair_ids = jnp.arange(HEAD_DIM // 2, dtype=jnp.int32)
    omegas = 100.0 ** ((pair_ids % quarter).astype(jnp.float32) / quarter)
    coord_all = jnp.where(pair_ids[None, :] < quarter, coord_y[:, None], coord_x[:, None])
    angles = jnp.where(is_patch[:, None], jnp.pi * omegas[None, :] * coord_all, 0.0)
    return (jnp.cos(angles), jnp.sin(angles))


def rotate(values, cos_rows, sin_rows):
    half_dim = values.shape[-1] // 2
    first_half = values[..., :half_dim]
    second_half = values[..., half_dim:]
    return jnp.concatenate(
        [
            first_half * cos_rows - second_half * sin_rows,
            second_half * cos_rows + first_half * sin_rows,
        ],
        axis=-1,
    )


def merge_sources(grid_row, merged_rows):
    heights, widths, starts, first_merged, last_merged = image_layout(grid_row)
    row_ids = jnp.arange(merged_rows, dtype=jnp.int32)
    onehot = (
        (row_ids[:, None] >= first_merged[None, :]) & (row_ids[:, None] < last_merged[None, :])
    ).astype(jnp.int32)
    is_valid = jnp.sum(onehot, axis=1) > 0
    row_width = pick_rows(onehot, widths)
    half_width = jnp.maximum(row_width // 2, 1)
    in_image = row_ids - pick_rows(onehot, first_merged)
    corner = (
        pick_rows(onehot, starts)
        + REG
        + 2 * (in_image // half_width) * row_width
        + 2 * (in_image % half_width)
    )
    offsets = jnp.stack(
        [jnp.zeros_like(row_width), jnp.ones_like(row_width), row_width, row_width + 1], axis=1
    )
    sources = jnp.where(is_valid[:, None], corner[:, None] + offsets, 0)
    return (sources, is_valid)


def owner_ranks(owner_row):
    count = owner_row.shape[0]
    same = owner_row[:, None] == owner_row[None, :]
    earlier = jnp.arange(count)[None, :] < jnp.arange(count)[:, None]
    return jnp.sum((same & earlier).astype(jnp.int32), axis=1)


def attention_body(query_ref, key_ref, value_ref, query_seg_ref, key_seg_ref, out_ref):
    scores = lax.dot_general(
        query_ref[...], key_ref[...], (((1,), (1,)), ((), ())), preferred_element_type=jnp.float32
    )
    scores = jnp.where(query_seg_ref[...] == key_seg_ref[...], scores, -jnp.inf)
    factor = HEAD_DIM ** (-0.5) * 1.4426950408889634
    top = jnp.max(scores, axis=1, keepdims=True)
    shifted = jnp.exp2((scores - top) * factor)
    total = jnp.sum(shifted, axis=1, keepdims=True)
    mixed = jnp.dot(
        shifted.astype(jnp.bfloat16), value_ref[...], preferred_element_type=jnp.float32
    )
    out_ref[...] = (mixed / total).astype(jnp.bfloat16)


def attention(qkv_rows, seg_row, local_heads):
    seq_len = qkv_rows.shape[0]
    block_len = min(512, seq_len)
    return pl.pallas_call(
        attention_body,
        grid=(local_heads, seq_len // block_len),
        out_shape=jax.ShapeDtypeStruct((seq_len, local_heads * HEAD_DIM), jnp.bfloat16),
        in_specs=[
            pl.BlockSpec((block_len, HEAD_DIM), lambda h, i: (i, h)),
            pl.BlockSpec((seq_len, HEAD_DIM), lambda h, i: (0, local_heads + h)),
            pl.BlockSpec((seq_len, HEAD_DIM), lambda h, i: (0, 2 * local_heads + h)),
            pl.BlockSpec((block_len, 1), lambda h, i: (i, 0)),
            pl.BlockSpec((1, seq_len), lambda h, i: (0, 0)),
        ],
        out_specs=pl.BlockSpec((block_len, HEAD_DIM), lambda h, i: (i, h)),
        compiler_params=pltpu.CompilerParams(vmem_limit_bytes=40 * 1024 * 1024),
    )(qkv_rows, qkv_rows, qkv_rows, seg_row[:, None], seg_row[None, :])


def local(
    tokens, ln_gain, ln_bias, w_qkv, w_out, layer_scale, w_merge, segment_ids, grid_sizes, owners
):
    tensor_count = lax.axis_size("tensor")
    batch_count = lax.axis_size("dp")
    seg_row = segment_ids[0]
    grid_row = grid_sizes[0]
    owner_row = owners[0, :, 0]
    seq_len = seg_row.shape[0]
    model_width = tokens.shape[2]
    col_width = layer_scale.shape[0]
    head_width = w_qkv.shape[2]
    local_heads = head_width // HEAD_DIM
    merged_rows = seq_len // 4
    device_count = batch_count * tensor_count
    own_cap = max(2, 3 * merged_rows // (2 * device_count))
    out_width = w_merge.shape[2]
    cos_table, sin_table = rope_tables(seg_row, grid_row, seq_len)
    qkv_weight = jnp.transpose(w_qkv, (1, 0, 2))
    all_tokens = lax.all_gather(tokens[0], "tensor", axis=0, tiled=True)
    normed = layer_norm(all_tokens, ln_gain, ln_bias)
    input_cols = lax.dynamic_slice_in_dim(
        all_tokens, lax.axis_index("tensor") * col_width, col_width, 1
    )
    count_rows = normed.shape[0]
    product = jnp.concatenate(
        [jnp.dot(normed, qkv_weight[n], preferred_element_type=jnp.float32) for n in range(3)], axis=1
    )
    cos_rows = cos_table[:, None, :]
    sin_rows = sin_table[:, None, :]
    query_part = rotate(
        product[:, :head_width].reshape(count_rows, local_heads, HEAD_DIM), cos_rows, sin_rows
    ).reshape(count_rows, head_width)
    key_part = rotate(
        product[:, head_width : 2 * head_width].reshape(count_rows, local_heads, HEAD_DIM),
        cos_rows,
        sin_rows,
    ).reshape(count_rows, head_width)
    qkv_rows = jnp.concatenate([query_part, key_part, product[:, 2 * head_width :]], axis=1).astype(
        jnp.bfloat16
    )[None][0]
    context = attention(qkv_rows, seg_row, local_heads)
    mixed = jnp.dot(
        lax.all_gather(context, "tensor", axis=1, tiled=True),
        w_out,
        preferred_element_type=jnp.float32,
    )
    hidden = (input_cols.astype(jnp.float32) + layer_scale * mixed).astype(jnp.bfloat16)
    sources, is_valid = merge_sources(grid_row, merged_rows)
    merge_weight = w_merge.reshape(4 * col_width, out_width)
    ranks = owner_ranks(owner_row)
    slot_keys = (
        (owner_row % tensor_count) * batch_count + owner_row // tensor_count
    ) * own_cap + ranks
    slot_ids = jnp.arange(device_count * own_cap, dtype=jnp.int32)
    placing = (slot_ids[:, None] == slot_keys[None, :]) & is_valid[None, :]
    positions = jnp.arange(seq_len, dtype=jnp.int32)
    picked = []
    for patch in range(4):
        source = jnp.sum(jnp.where(placing, sources[:, patch][None, :] + 1, 0), axis=1) - 1
        onehot = (source[:, None] == positions[None, :]).astype(jnp.bfloat16)
        picked.append(
            jnp.dot(onehot, hidden, preferred_element_type=jnp.float32).astype(jnp.bfloat16)
        )
    by_owner = jnp.concatenate(picked, axis=1)
    group_part = jnp.dot(by_owner, merge_weight, preferred_element_type=jnp.float32).astype(
        jnp.bfloat16
    )
    owned = lax.psum_scatter(group_part, "tensor", scatter_dimension=0, tiled=True)
    arrived = lax.all_to_all(
        owned.reshape(batch_count, own_cap, out_width), "dp", split_axis=0, concat_axis=0, tiled=True
    )
    return arrived.reshape(1, batch_count * own_cap, out_width)


def solution(mesh):
    in_specs = (
        P("dp", "tensor", None),
        P(),
        P(),
        P(None, None, "tensor"),
        P(None, "tensor"),
        P("tensor"),
        P(None, "tensor", None),
        P("dp", None),
        P("dp", None, None),
        P("dp", None, None),
    )
    out_specs = P("dp", "tensor", None)
    return jax.shard_map(local, mesh=mesh, in_specs=in_specs, out_specs=out_specs, check_vma=False)
```

```python
import functools

import jax
import jax.numpy as jnp
from jax import lax
from jax.experimental import pallas as pl
from jax.experimental.pallas import tpu as pltpu
from jax.sharding import PartitionSpec as P

HEAD_DIM = 128
IMGS = 3
REG = 5


norm_eps = 1e-06


def layer_norm(row_data, gain_vec, shift_vec):
    values = row_data.astype(jnp.float32)
    center = values - jnp.mean(values, axis=-1, keepdims=True)
    spread = jnp.mean(center * center, axis=-1, keepdims=True)
    return (center * lax.rsqrt(spread + norm_eps) * gain_vec + shift_vec).astype(jnp.bfloat16)


def running_sum(values):
    count = values.shape[0]
    lower = jnp.arange(count)[:, None] >= jnp.arange(count)[None, :]
    return jnp.sum(jnp.where(lower, values[None, :], 0), axis=1)


def image_layout(grid_row):
    heights = grid_row[:, 0]
    widths = grid_row[:, 1]
    lengths = REG + heights * widths
    starts = running_sum(lengths) - lengths
    counts = heights // 2 * (widths // 2)
    merged_end = running_sum(counts)
    return (heights, widths, starts, merged_end - counts, merged_end)


def pick_rows(onehot, lookup):
    return jnp.sum(onehot * lookup[None, :], axis=1)


def rope_tables(seg_row, grid_row, seq_len):
    heights, widths, starts, first_merged, last_merged = image_layout(grid_row)
    position = jnp.arange(seq_len, dtype=jnp.int32)
    image_ids = jnp.arange(IMGS, dtype=jnp.int32)
    onehot = (seg_row[:, None] == image_ids[None, :]).astype(jnp.int32)
    is_image = jnp.sum(onehot, axis=1) > 0
    in_image = position - pick_rows(onehot, starts) - REG
    is_patch = is_image & (in_image >= 0)
    row_width = jnp.maximum(pick_rows(onehot, widths), 1)
    col_height = jnp.maximum(pick_rows(onehot, heights), 1)
    clipped = jnp.maximum(in_image, 0)
    coord_y = (
        2.0 * ((clipped // row_width).astype(jnp.float32) + 0.5) / col_height.astype(jnp.float32)
        - 1.0
    )
    coord_x = (
        2.0 * ((clipped % row_width).astype(jnp.float32) + 0.5) / row_width.astype(jnp.float32)
        - 1.0
    )
    quarter = HEAD_DIM // 4
    pair_ids = jnp.arange(HEAD_DIM // 2, dtype=jnp.int32)
    omegas = 100.0 ** ((pair_ids % quarter).astype(jnp.float32) / quarter)
    coord_all = jnp.where(pair_ids[None, :] < quarter, coord_y[:, None], coord_x[:, None])
    angles = jnp.where(is_patch[:, None], jnp.pi * omegas[None, :] * coord_all, 0.0)
    return (jnp.cos(angles), jnp.sin(angles))


def rotate(values, cos_rows, sin_rows):
    half_dim = values.shape[-1] // 2
    first_half = values[..., :half_dim]
    second_half = values[..., half_dim:]
    return jnp.concatenate(
        [
            first_half * cos_rows - second_half * sin_rows,
            second_half * cos_rows + first_half * sin_rows,
        ],
        axis=-1,
    )


def merge_sources(grid_row, merged_rows):
    heights, widths, starts, first_merged, last_merged = image_layout(grid_row)
    row_ids = jnp.arange(merged_rows, dtype=jnp.int32)
    onehot = (
        (row_ids[:, None] >= first_merged[None, :]) & (row_ids[:, None] < last_merged[None, :])
    ).astype(jnp.int32)
    is_valid = jnp.sum(onehot, axis=1) > 0
    row_width = pick_rows(onehot, widths)
    half_width = jnp.maximum(row_width // 2, 1)
    in_image = row_ids - pick_rows(onehot, first_merged)
    corner = (
        pick_rows(onehot, starts)
        + REG
        + 2 * (in_image // half_width) * row_width
        + 2 * (in_image % half_width)
    )
    offsets = jnp.stack(
        [jnp.zeros_like(row_width), jnp.ones_like(row_width), row_width, row_width + 1], axis=1
    )
    sources = jnp.where(is_valid[:, None], corner[:, None] + offsets, 0)
    return (sources, is_valid)


def owner_ranks(owner_row):
    count = owner_row.shape[0]
    same = owner_row[:, None] == owner_row[None, :]
    earlier = jnp.arange(count)[None, :] < jnp.arange(count)[:, None]
    return jnp.sum((same & earlier).astype(jnp.int32), axis=1)


def attention_body(query_ref, key_ref, value_ref, query_seg_ref, key_seg_ref, out_ref):
    scores = lax.dot_general(
        query_ref[...], key_ref[...], (((1,), (1,)), ((), ())), preferred_element_type=jnp.float32
    )
    scores = jnp.where(query_seg_ref[...] == key_seg_ref[...], scores, -jnp.inf)
    factor = HEAD_DIM ** (-0.5) * 1.4426950408889634
    top = jnp.max(scores, axis=1, keepdims=True)
    shifted = jnp.exp2((scores - top) * factor)
    total = jnp.sum(shifted, axis=1, keepdims=True)
    mixed = jnp.dot(
        shifted.astype(jnp.bfloat16), value_ref[...], preferred_element_type=jnp.float32
    )
    out_ref[...] = (mixed / total).astype(jnp.bfloat16)


def attention(qkv_rows, seg_row, local_heads):
    seq_len = qkv_rows.shape[0]
    block_len = min(512, seq_len)
    return pl.pallas_call(
        attention_body,
        grid=(local_heads, seq_len // block_len),
        out_shape=jax.ShapeDtypeStruct((seq_len, local_heads * HEAD_DIM), jnp.bfloat16),
        in_specs=[
            pl.BlockSpec((block_len, HEAD_DIM), lambda h, i: (i, h)),
            pl.BlockSpec((seq_len, HEAD_DIM), lambda h, i: (0, local_heads + h)),
            pl.BlockSpec((seq_len, HEAD_DIM), lambda h, i: (0, 2 * local_heads + h)),
            pl.BlockSpec((block_len, 1), lambda h, i: (i, 0)),
            pl.BlockSpec((1, seq_len), lambda h, i: (0, 0)),
        ],
        out_specs=pl.BlockSpec((block_len, HEAD_DIM), lambda h, i: (i, h)),
        compiler_params=pltpu.CompilerParams(vmem_limit_bytes=40 * 1024 * 1024),
    )(qkv_rows, qkv_rows, qkv_rows, seg_row[:, None], seg_row[None, :])


MESH = pl.DeviceIdType.MESH


def flipped(me, slot):
    result = 0
    for bit in (1, 2, 4):
        mine, other = lax.rem(lax.div(me, bit), 2), lax.rem(lax.div(slot, bit), 2)
        result = result + bit * (mine + other - 2 * mine * other)
    return result


def greet(me):
    barrier = pltpu.get_barrier_semaphore()
    for bit in (1, 2, 4):
        peer = me + bit - 2 * bit * lax.rem(lax.div(me, bit), 2)
        pl.semaphore_signal(barrier, inc=1, device_id={"tensor": peer}, device_id_type=MESH)
    pl.semaphore_wait(barrier, 3)


def sender(me, own_ref, held, send_sem, recv_sem):
    def copy(slot, half):
        if slot in (1, 3, 5, 7):
            bit, source = 1, slot - 1
        elif slot == 6:
            bit, source = (4, 2) if half == 0 else (2, 4)
        else:
            bit, source = slot, 0
        peer = me + bit - 2 * bit * lax.rem(lax.div(me, bit), 2)
        return pltpu.make_async_remote_copy(
            src_ref=own_ref.at[half] if source == 0 else held.at[source, half],
            dst_ref=held.at[slot, half],
            send_sem=send_sem.at[slot, half],
            recv_sem=recv_sem.at[slot, half],
            device_id={"tensor": peer},
            device_id_type=MESH,
        )

    return copy


def gather_phases(copy, compute):
    copy(1, 0).wait_recv()
    copy(1, 1).wait_recv()
    compute(0, 2)
    copy(2, 0).wait_recv()
    copy(6, 0).start()
    copy(3, 0).start()
    copy(4, 1).wait_recv()
    copy(6, 1).start()
    copy(5, 1).start()
    copy(2, 1).wait_recv()
    copy(3, 1).start()
    copy(4, 0).wait_recv()
    copy(5, 0).start()
    for slot in (3, 5):
        for half in (0, 1):
            copy(slot, half).wait_recv()
    compute(2, 6)
    for half in (0, 1):
        copy(6, half).wait_recv()
        copy(7, half).start()
    for half in (0, 1):
        copy(7, half).wait_recv()
    compute(6, 8)
    for slot in range(1, 8):
        for half in (0, 1):
            copy(slot, half).wait_send()


def project_body(
    x_ref, gain_ref, bias_ref, cos_ref, sin_ref, w_hbm, qkv_ref, cols_ref,
    held, normed, weight, send_sem, recv_sem, load_sem,
):
    me = lax.axis_index("tensor")
    load = pltpu.make_async_copy(w_hbm, weight, load_sem)
    load.start()
    greet(me)
    copy = sender(me, x_ref, held, send_sem, recv_sem)
    for slot, half in ((2, 0), (4, 1), (1, 0), (1, 1), (2, 1), (4, 0)):
        copy(slot, half).start()
    held[0] = x_ref[...]
    load.wait()
    half_rows, head_width = held.shape[2], weight.shape[2]
    rows = 2 * half_rows
    own_cols = pl.ds(pl.multiple_of(me * head_width, head_width), head_width)

    def one_slot(slot, carry):
        first = pl.multiple_of(flipped(me, slot) * rows, rows)
        for half in range(2):

            def one_strip(strip, inner):
                start = pl.multiple_of(strip * 16, 16)
                values = held[slot, half, pl.ds(start, 16), :].astype(jnp.float32)
                center = values - jnp.mean(values, axis=1, keepdims=True)
                spread = jnp.mean(center * center, axis=1, keepdims=True)
                normal = center * lax.rsqrt(spread + norm_eps) * gain_ref[...] + bias_ref[...]
                normed[pl.ds(pl.multiple_of(half * half_rows + start, 16), 16), :] = normal.astype(
                    jnp.bfloat16
                )
                return inner

            lax.fori_loop(0, half_rows // 16, one_strip, 0)
            cols_ref[pl.ds(pl.multiple_of(first + half * half_rows, 16), half_rows), :] = held[
                slot, half, :, own_cols
            ]
        cos_rows = cos_ref[pl.ds(first, rows), :]
        sin_rows = sin_ref[pl.ds(first, rows), :]
        for part in range(3):
            product = jnp.dot(normed[...], weight[part], preferred_element_type=jnp.float32)
            for head in range(head_width // HEAD_DIM):
                piece = product[:, head * HEAD_DIM : (head + 1) * HEAD_DIM]
                if part < 2:
                    piece = piece * cos_rows + pltpu.roll(piece, HEAD_DIM // 2, 1) * sin_rows
                start = part * head_width + head * HEAD_DIM
                qkv_ref[pl.ds(first, rows), start : start + HEAD_DIM] = piece.astype(jnp.bfloat16)
        return carry

    gather_phases(copy, lambda low, high: lax.fori_loop(low, high, one_slot, 0))


def project(tokens, ln_gain, ln_bias, cos_table, sin_table, w_qkv):
    rows, width = tokens.shape
    head_width = w_qkv.shape[2]
    seq_len = 8 * rows
    vmem = pl.BlockSpec(memory_space=pltpu.VMEM)
    return pl.pallas_call(
        project_body,
        out_shape=(
            jax.ShapeDtypeStruct((seq_len, 3 * head_width), jnp.bfloat16),
            jax.ShapeDtypeStruct((seq_len, head_width), jnp.bfloat16),
        ),
        in_specs=[vmem] * 5 + [pl.BlockSpec(memory_space=pl.ANY)],
        out_specs=(vmem, vmem),
        scratch_shapes=[
            pltpu.VMEM((8, 2, rows // 2, width), jnp.bfloat16),
            pltpu.VMEM((rows, width), jnp.bfloat16),
            pltpu.VMEM((3, width, head_width), jnp.bfloat16),
            pltpu.SemaphoreType.DMA((8, 2)),
            pltpu.SemaphoreType.DMA((8, 2)),
            pltpu.SemaphoreType.DMA,
        ],
        compiler_params=pltpu.CompilerParams(
            collective_id=0, has_side_effects=True, vmem_limit_bytes=56 * 1024 * 1024
        ),
    )(
        tokens.reshape(2, rows // 2, width),
        ln_gain[None, :],
        ln_bias[None, :],
        jnp.concatenate([cos_table, cos_table], axis=1),
        jnp.concatenate([-sin_table, sin_table], axis=1),
        jnp.transpose(w_qkv, (1, 0, 2)),
    )


def mix_body(
    qkv_ref, query_seg_ref, key_seg_ref, cols_ref, scale_ref, w_hbm, out_ref,
    held, total, weight, send_sem, recv_sem, load_sem,
):
    me = lax.axis_index("tensor")
    load = pltpu.make_async_copy(w_hbm, weight, load_sem)
    load.start()
    greet(me)
    copy = sender(me, held.at[0], held, send_sem, recv_sem)
    seq_len, head_width = cols_ref.shape
    block = min(256, seq_len)
    factor = HEAD_DIM ** (-0.5) * 1.4426950408889634

    def one_block(half, index, carry):
        rows = pl.ds(pl.multiple_of(index * block, block), block)
        same = query_seg_ref[rows, :] == key_seg_ref[...]
        for place in range(2):
            start = (half * 2 + place) * HEAD_DIM
            query = qkv_ref[rows, start : start + HEAD_DIM]
            key = qkv_ref[:, head_width + start : head_width + start + HEAD_DIM]
            value = qkv_ref[:, 2 * head_width + start : 2 * head_width + start + HEAD_DIM]
            scores = lax.dot_general(
                query, key, (((1,), (1,)), ((), ())), preferred_element_type=jnp.float32
            )
            scores = jnp.where(same, scores, -jnp.inf)
            top = jnp.max(scores, axis=1, keepdims=True)
            shifted = jnp.exp2((scores - top) * factor)
            weights_sum = jnp.sum(shifted, axis=1, keepdims=True)
            mixed = jnp.dot(shifted.astype(jnp.bfloat16), value, preferred_element_type=jnp.float32)
            held[0, half, rows, place * HEAD_DIM : (place + 1) * HEAD_DIM] = (
                mixed / weights_sum
            ).astype(jnp.bfloat16)
        return carry

    for half in range(2):
        lax.fori_loop(0, seq_len // block, functools.partial(one_block, half), 0)
        for slot in (2, 4, 1):
            copy(slot, half).start()
    total[...] = jnp.zeros_like(total)
    load.wait()

    def one_slot(slot, carry):
        source = flipped(me, slot)
        for index in range(seq_len // 512):
            rows = pl.ds(index * 512, 512)
            total[rows, :] += jnp.dot(
                held[slot, 0, rows, :], weight[2 * source], preferred_element_type=jnp.float32
            ) + jnp.dot(
                held[slot, 1, rows, :], weight[2 * source + 1], preferred_element_type=jnp.float32
            )
        return carry

    gather_phases(copy, lambda low, high: lax.fori_loop(low, high, one_slot, 0))
    out_ref[...] = (cols_ref[...].astype(jnp.float32) + scale_ref[...] * total[...]).astype(
        jnp.bfloat16
    )


def mix(qkv_rows, seg_row, input_cols, layer_scale, w_out):
    seq_len, head_width = input_cols.shape
    vmem = pl.BlockSpec(memory_space=pltpu.VMEM)
    return pl.pallas_call(
        mix_body,
        out_shape=jax.ShapeDtypeStruct((seq_len, head_width), jnp.bfloat16),
        in_specs=[vmem] * 5 + [pl.BlockSpec(memory_space=pl.ANY)],
        out_specs=vmem,
        scratch_shapes=[
            pltpu.VMEM((8, 2, seq_len, 2 * HEAD_DIM), jnp.bfloat16),
            pltpu.VMEM((seq_len, head_width), jnp.float32),
            pltpu.VMEM((16, 2 * HEAD_DIM, head_width), jnp.bfloat16),
            pltpu.SemaphoreType.DMA((8, 2)),
            pltpu.SemaphoreType.DMA((8, 2)),
            pltpu.SemaphoreType.DMA,
        ],
        compiler_params=pltpu.CompilerParams(
            collective_id=1, has_side_effects=True, vmem_limit_bytes=56 * 1024 * 1024
        ),
    )(
        qkv_rows,
        seg_row[:, None],
        seg_row[None, :],
        input_cols,
        layer_scale[None, :],
        w_out.reshape(16, 2 * HEAD_DIM, head_width),
    )


def general_hidden(
    tokens, ln_gain, ln_bias, cos_table, sin_table, w_qkv, seg_row, layer_scale, w_out
):
    model_width = tokens.shape[2]
    col_width = layer_scale.shape[0]
    head_width = w_qkv.shape[2]
    local_heads = head_width // HEAD_DIM
    qkv_weight = jnp.transpose(w_qkv, (1, 0, 2))
    all_tokens = lax.all_gather(tokens[0], "tensor", axis=0, tiled=True)
    normed = layer_norm(all_tokens, ln_gain, ln_bias)
    input_cols = lax.dynamic_slice_in_dim(
        all_tokens, lax.axis_index("tensor") * col_width, col_width, 1
    )
    count_rows = normed.shape[0]
    product = jnp.concatenate(
        [jnp.dot(normed, qkv_weight[n], preferred_element_type=jnp.float32) for n in range(3)], axis=1
    )
    cos_rows = cos_table[:, None, :]
    sin_rows = sin_table[:, None, :]
    query_part = rotate(
        product[:, :head_width].reshape(count_rows, local_heads, HEAD_DIM), cos_rows, sin_rows
    ).reshape(count_rows, head_width)
    key_part = rotate(
        product[:, head_width : 2 * head_width].reshape(count_rows, local_heads, HEAD_DIM),
        cos_rows,
        sin_rows,
    ).reshape(count_rows, head_width)
    qkv_rows = jnp.concatenate([query_part, key_part, product[:, 2 * head_width :]], axis=1).astype(
        jnp.bfloat16
    )[None][0]
    context = attention(qkv_rows, seg_row, local_heads)
    mixed = jnp.dot(
        lax.all_gather(context, "tensor", axis=1, tiled=True),
        w_out,
        preferred_element_type=jnp.float32,
    )
    hidden = (input_cols.astype(jnp.float32) + layer_scale * mixed).astype(jnp.bfloat16)
    return hidden


def local(
    tokens, ln_gain, ln_bias, w_qkv, w_out, layer_scale, w_merge, segment_ids, grid_sizes, owners
):
    tensor_count = lax.axis_size("tensor")
    batch_count = lax.axis_size("dp")
    seg_row = segment_ids[0]
    grid_row = grid_sizes[0]
    owner_row = owners[0, :, 0]
    seq_len = seg_row.shape[0]
    model_width = tokens.shape[2]
    col_width = layer_scale.shape[0]
    head_width = w_qkv.shape[2]
    local_heads = head_width // HEAD_DIM
    merged_rows = seq_len // 4
    device_count = batch_count * tensor_count
    own_cap = max(2, 3 * merged_rows // (2 * device_count))
    out_width = w_merge.shape[2]
    cos_table, sin_table = rope_tables(seg_row, grid_row, seq_len)
    if tensor_count == 8 and head_width == 4 * HEAD_DIM and col_width == head_width:
        qkv_rows, input_cols = project(tokens[0], ln_gain, ln_bias, cos_table, sin_table, w_qkv)
        hidden = mix(qkv_rows, seg_row, input_cols, layer_scale, w_out)
    else:
        hidden = general_hidden(
            tokens, ln_gain, ln_bias, cos_table, sin_table, w_qkv, seg_row, layer_scale, w_out
        )
    sources, is_valid = merge_sources(grid_row, merged_rows)
    merge_weight = w_merge.reshape(4 * col_width, out_width)
    ranks = owner_ranks(owner_row)
    slot_keys = (
        (owner_row % tensor_count) * batch_count + owner_row // tensor_count
    ) * own_cap + ranks
    slot_ids = jnp.arange(device_count * own_cap, dtype=jnp.int32)
    placing = (slot_ids[:, None] == slot_keys[None, :]) & is_valid[None, :]
    positions = jnp.arange(seq_len, dtype=jnp.int32)
    picked = []
    for patch in range(4):
        source = jnp.sum(jnp.where(placing, sources[:, patch][None, :] + 1, 0), axis=1) - 1
        onehot = (source[:, None] == positions[None, :]).astype(jnp.bfloat16)
        picked.append(
            jnp.dot(onehot, hidden, preferred_element_type=jnp.float32).astype(jnp.bfloat16)
        )
    by_owner = jnp.concatenate(picked, axis=1)
    group_part = jnp.dot(by_owner, merge_weight, preferred_element_type=jnp.float32).astype(
        jnp.bfloat16
    )
    owned = lax.psum_scatter(group_part, "tensor", scatter_dimension=0, tiled=True)
    arrived = lax.all_to_all(
        owned.reshape(batch_count, own_cap, out_width), "dp", split_axis=0, concat_axis=0, tiled=True
    )
    return arrived.reshape(1, batch_count * own_cap, out_width)


def solution(mesh):
    in_specs = (
        P("dp", "tensor", None),
        P(),
        P(),
        P(None, None, "tensor"),
        P(None, "tensor"),
        P("tensor"),
        P(None, "tensor", None),
        P("dp", None),
        P("dp", None, None),
        P("dp", None, None),
    )
    out_specs = P("dp", "tensor", None)
    return jax.shard_map(local, mesh=mesh, in_specs=in_specs, out_specs=out_specs, check_vma=False)
```

```python
import functools

import jax
import jax.numpy as jnp
from jax import lax
from jax.experimental import pallas as pl
from jax.experimental.pallas import tpu as pltpu
from jax.sharding import PartitionSpec as P

HEAD_DIM = 128
IMGS = 3
REG = 5


norm_eps = 1e-06


def layer_norm(row_data, gain_vec, shift_vec):
    values = row_data.astype(jnp.float32)
    center = values - jnp.mean(values, axis=-1, keepdims=True)
    spread = jnp.mean(center * center, axis=-1, keepdims=True)
    return (center * lax.rsqrt(spread + norm_eps) * gain_vec + shift_vec).astype(jnp.bfloat16)


def running_sum(values):
    count = values.shape[0]
    lower = jnp.arange(count)[:, None] >= jnp.arange(count)[None, :]
    return jnp.sum(jnp.where(lower, values[None, :], 0), axis=1)


def image_layout(grid_row):
    heights = grid_row[:, 0]
    widths = grid_row[:, 1]
    lengths = REG + heights * widths
    starts = running_sum(lengths) - lengths
    counts = heights // 2 * (widths // 2)
    merged_end = running_sum(counts)
    return (heights, widths, starts, merged_end - counts, merged_end)


def pick_rows(onehot, lookup):
    return jnp.sum(onehot * lookup[None, :], axis=1)


def rope_tables(seg_row, grid_row, seq_len):
    heights, widths, starts, first_merged, last_merged = image_layout(grid_row)
    position = jnp.arange(seq_len, dtype=jnp.int32)
    image_ids = jnp.arange(IMGS, dtype=jnp.int32)
    onehot = (seg_row[:, None] == image_ids[None, :]).astype(jnp.int32)
    is_image = jnp.sum(onehot, axis=1) > 0
    in_image = position - pick_rows(onehot, starts) - REG
    is_patch = is_image & (in_image >= 0)
    row_width = jnp.maximum(pick_rows(onehot, widths), 1)
    col_height = jnp.maximum(pick_rows(onehot, heights), 1)
    clipped = jnp.maximum(in_image, 0)
    coord_y = (
        2.0 * ((clipped // row_width).astype(jnp.float32) + 0.5) / col_height.astype(jnp.float32)
        - 1.0
    )
    coord_x = (
        2.0 * ((clipped % row_width).astype(jnp.float32) + 0.5) / row_width.astype(jnp.float32)
        - 1.0
    )
    quarter = HEAD_DIM // 4
    pair_ids = jnp.arange(HEAD_DIM // 2, dtype=jnp.int32)
    omegas = 100.0 ** ((pair_ids % quarter).astype(jnp.float32) / quarter)
    coord_all = jnp.where(pair_ids[None, :] < quarter, coord_y[:, None], coord_x[:, None])
    angles = jnp.where(is_patch[:, None], jnp.pi * omegas[None, :] * coord_all, 0.0)
    return (jnp.cos(angles), jnp.sin(angles))


def rotate(values, cos_rows, sin_rows):
    half_dim = values.shape[-1] // 2
    first_half = values[..., :half_dim]
    second_half = values[..., half_dim:]
    return jnp.concatenate(
        [
            first_half * cos_rows - second_half * sin_rows,
            second_half * cos_rows + first_half * sin_rows,
        ],
        axis=-1,
    )


def merge_sources(grid_row, merged_rows):
    heights, widths, starts, first_merged, last_merged = image_layout(grid_row)
    row_ids = jnp.arange(merged_rows, dtype=jnp.int32)
    onehot = (
        (row_ids[:, None] >= first_merged[None, :]) & (row_ids[:, None] < last_merged[None, :])
    ).astype(jnp.int32)
    is_valid = jnp.sum(onehot, axis=1) > 0
    row_width = pick_rows(onehot, widths)
    half_width = jnp.maximum(row_width // 2, 1)
    in_image = row_ids - pick_rows(onehot, first_merged)
    corner = (
        pick_rows(onehot, starts)
        + REG
        + 2 * (in_image // half_width) * row_width
        + 2 * (in_image % half_width)
    )
    offsets = jnp.stack(
        [jnp.zeros_like(row_width), jnp.ones_like(row_width), row_width, row_width + 1], axis=1
    )
    sources = jnp.where(is_valid[:, None], corner[:, None] + offsets, 0)
    return (sources, is_valid)


def owner_ranks(owner_row):
    count = owner_row.shape[0]
    same = owner_row[:, None] == owner_row[None, :]
    earlier = jnp.arange(count)[None, :] < jnp.arange(count)[:, None]
    return jnp.sum((same & earlier).astype(jnp.int32), axis=1)


def attention_body(query_ref, key_ref, value_ref, query_seg_ref, key_seg_ref, out_ref):
    scores = lax.dot_general(
        query_ref[...], key_ref[...], (((1,), (1,)), ((), ())), preferred_element_type=jnp.float32
    )
    scores = jnp.where(query_seg_ref[...] == key_seg_ref[...], scores, -jnp.inf)
    factor = HEAD_DIM ** (-0.5) * 1.4426950408889634
    top = jnp.max(scores, axis=1, keepdims=True)
    shifted = jnp.exp2((scores - top) * factor)
    total = jnp.sum(shifted, axis=1, keepdims=True)
    mixed = jnp.dot(
        shifted.astype(jnp.bfloat16), value_ref[...], preferred_element_type=jnp.float32
    )
    out_ref[...] = (mixed / total).astype(jnp.bfloat16)


def attention(qkv_rows, seg_row, local_heads):
    seq_len = qkv_rows.shape[0]
    block_len = min(512, seq_len)
    return pl.pallas_call(
        attention_body,
        grid=(local_heads, seq_len // block_len),
        out_shape=jax.ShapeDtypeStruct((seq_len, local_heads * HEAD_DIM), jnp.bfloat16),
        in_specs=[
            pl.BlockSpec((block_len, HEAD_DIM), lambda h, i: (i, h)),
            pl.BlockSpec((seq_len, HEAD_DIM), lambda h, i: (0, local_heads + h)),
            pl.BlockSpec((seq_len, HEAD_DIM), lambda h, i: (0, 2 * local_heads + h)),
            pl.BlockSpec((block_len, 1), lambda h, i: (i, 0)),
            pl.BlockSpec((1, seq_len), lambda h, i: (0, 0)),
        ],
        out_specs=pl.BlockSpec((block_len, HEAD_DIM), lambda h, i: (i, h)),
        compiler_params=pltpu.CompilerParams(vmem_limit_bytes=40 * 1024 * 1024),
    )(qkv_rows, qkv_rows, qkv_rows, seg_row[:, None], seg_row[None, :])


MESH = pl.DeviceIdType.MESH


def flipped(me, slot):
    result = 0
    for bit in (1, 2, 4):
        mine, other = lax.rem(lax.div(me, bit), 2), lax.rem(lax.div(slot, bit), 2)
        result = result + bit * (mine + other - 2 * mine * other)
    return result


def greet(me):
    barrier = pltpu.get_barrier_semaphore()
    for bit in (1, 2, 4):
        peer = me + bit - 2 * bit * lax.rem(lax.div(me, bit), 2)
        pl.semaphore_signal(barrier, inc=1, device_id={"tensor": peer}, device_id_type=MESH)
    pl.semaphore_wait(barrier, 3)


def sender(me, own_ref, held, send_sem, recv_sem):
    def copy(slot, half):
        if slot in (1, 3, 5, 7):
            bit, source = 1, slot - 1
        elif slot == 6:
            bit, source = (4, 2) if half == 0 else (2, 4)
        else:
            bit, source = slot, 0
        peer = me + bit - 2 * bit * lax.rem(lax.div(me, bit), 2)
        return pltpu.make_async_remote_copy(
            src_ref=own_ref.at[half] if source == 0 else held.at[source, half],
            dst_ref=held.at[slot, half],
            send_sem=send_sem.at[slot, half],
            recv_sem=recv_sem.at[slot, half],
            device_id={"tensor": peer},
            device_id_type=MESH,
        )

    return copy


def gather_phases(copy, compute):
    copy(1, 0).wait_recv()
    copy(1, 1).wait_recv()
    compute(0, 2)
    copy(2, 0).wait_recv()
    copy(6, 0).start()
    copy(3, 0).start()
    copy(4, 1).wait_recv()
    copy(6, 1).start()
    copy(5, 1).start()
    copy(2, 1).wait_recv()
    copy(3, 1).start()
    copy(4, 0).wait_recv()
    copy(5, 0).start()
    for slot in (3, 5):
        for half in (0, 1):
            copy(slot, half).wait_recv()
    compute(2, 6)
    for half in (0, 1):
        copy(6, half).wait_recv()
        copy(7, half).start()
    for half in (0, 1):
        copy(7, half).wait_recv()
    compute(6, 8)
    for slot in range(1, 8):
        for half in (0, 1):
            copy(slot, half).wait_send()


def project_body(
    x_ref, gain_ref, bias_ref, cos_ref, sin_ref, w_hbm, qkv_ref, cols_ref,
    held, normed, weight, send_sem, recv_sem, load_sem,
):
    me = lax.axis_index("tensor")
    load = pltpu.make_async_copy(w_hbm, weight, load_sem)
    load.start()
    greet(me)
    copy = sender(me, x_ref, held, send_sem, recv_sem)
    for slot, half in ((2, 0), (4, 1), (1, 0), (1, 1), (2, 1), (4, 0)):
        copy(slot, half).start()
    held[0] = x_ref[...]
    load.wait()
    half_rows, head_width = held.shape[2], weight.shape[2]
    rows = 2 * half_rows
    own_cols = pl.ds(pl.multiple_of(me * head_width, head_width), head_width)

    def one_slot(slot, carry):
        first = pl.multiple_of(flipped(me, slot) * rows, rows)
        for half in range(2):

            def one_strip(strip, inner):
                start = pl.multiple_of(strip * 16, 16)
                values = held[slot, half, pl.ds(start, 16), :].astype(jnp.float32)
                center = values - jnp.mean(values, axis=1, keepdims=True)
                spread = jnp.mean(center * center, axis=1, keepdims=True)
                normal = center * lax.rsqrt(spread + norm_eps) * gain_ref[...] + bias_ref[...]
                normed[pl.ds(pl.multiple_of(half * half_rows + start, 16), 16), :] = normal.astype(
                    jnp.bfloat16
                )
                return inner

            lax.fori_loop(0, half_rows // 16, one_strip, 0)
            cols_ref[pl.ds(pl.multiple_of(first + half * half_rows, 16), half_rows), :] = held[
                slot, half, :, own_cols
            ]
        cos_rows = cos_ref[pl.ds(first, rows), :]
        sin_rows = sin_ref[pl.ds(first, rows), :]
        for part in range(3):
            product = jnp.dot(normed[...], weight[part], preferred_element_type=jnp.float32)
            for head in range(head_width // HEAD_DIM):
                piece = product[:, head * HEAD_DIM : (head + 1) * HEAD_DIM]
                if part < 2:
                    piece = piece * cos_rows + pltpu.roll(piece, HEAD_DIM // 2, 1) * sin_rows
                start = part * head_width + head * HEAD_DIM
                qkv_ref[pl.ds(first, rows), start : start + HEAD_DIM] = piece.astype(jnp.bfloat16)
        return carry

    gather_phases(copy, lambda low, high: lax.fori_loop(low, high, one_slot, 0))


def project(tokens, ln_gain, ln_bias, cos_table, sin_table, w_qkv):
    rows, width = tokens.shape
    head_width = w_qkv.shape[2]
    seq_len = 8 * rows
    vmem = pl.BlockSpec(memory_space=pltpu.VMEM)
    return pl.pallas_call(
        project_body,
        out_shape=(
            jax.ShapeDtypeStruct((seq_len, 3 * head_width), jnp.bfloat16),
            jax.ShapeDtypeStruct((seq_len, head_width), jnp.bfloat16),
        ),
        in_specs=[vmem] * 5 + [pl.BlockSpec(memory_space=pl.ANY)],
        out_specs=(vmem, vmem),
        scratch_shapes=[
            pltpu.VMEM((8, 2, rows // 2, width), jnp.bfloat16),
            pltpu.VMEM((rows, width), jnp.bfloat16),
            pltpu.VMEM((3, width, head_width), jnp.bfloat16),
            pltpu.SemaphoreType.DMA((8, 2)),
            pltpu.SemaphoreType.DMA((8, 2)),
            pltpu.SemaphoreType.DMA,
        ],
        compiler_params=pltpu.CompilerParams(
            collective_id=0, has_side_effects=True, vmem_limit_bytes=56 * 1024 * 1024
        ),
    )(
        tokens.reshape(2, rows // 2, width),
        ln_gain[None, :],
        ln_bias[None, :],
        jnp.concatenate([cos_table, cos_table], axis=1),
        jnp.concatenate([-sin_table, sin_table], axis=1),
        jnp.transpose(w_qkv, (1, 0, 2)),
    )


def mix_body(
    qkv_ref, query_seg_ref, key_seg_ref, cols_ref, scale_ref, w_hbm, out_ref,
    held, total, weight, send_sem, recv_sem, load_sem,
):
    me = lax.axis_index("tensor")
    load = pltpu.make_async_copy(w_hbm, weight, load_sem)
    load.start()
    greet(me)
    copy = sender(me, held.at[0], held, send_sem, recv_sem)
    seq_len, head_width = cols_ref.shape
    block = min(256, seq_len)
    factor = HEAD_DIM ** (-0.5) * 1.4426950408889634

    def one_block(half, index, carry):
        rows = pl.ds(pl.multiple_of(index * block, block), block)
        same = query_seg_ref[rows, :] == key_seg_ref[...]
        for place in range(2):
            start = (half * 2 + place) * HEAD_DIM
            query = qkv_ref[rows, start : start + HEAD_DIM]
            key = qkv_ref[:, head_width + start : head_width + start + HEAD_DIM]
            value = qkv_ref[:, 2 * head_width + start : 2 * head_width + start + HEAD_DIM]
            scores = lax.dot_general(
                query, key, (((1,), (1,)), ((), ())), preferred_element_type=jnp.float32
            )
            scores = jnp.where(same, scores, -jnp.inf)
            top = jnp.max(scores, axis=1, keepdims=True)
            shifted = jnp.exp2((scores - top) * factor)
            weights_sum = jnp.sum(shifted, axis=1, keepdims=True)
            mixed = jnp.dot(shifted.astype(jnp.bfloat16), value, preferred_element_type=jnp.float32)
            held[0, half, rows, place * HEAD_DIM : (place + 1) * HEAD_DIM] = (
                mixed / weights_sum
            ).astype(jnp.bfloat16)
        return carry

    for half in range(2):
        lax.fori_loop(0, seq_len // block, functools.partial(one_block, half), 0)
        for slot in (2, 4, 1):
            copy(slot, half).start()
    total[...] = jnp.zeros_like(total)
    load.wait()

    def one_slot(slot, carry):
        source = flipped(me, slot)
        for index in range(seq_len // 512):
            rows = pl.ds(index * 512, 512)
            total[rows, :] += jnp.dot(
                held[slot, 0, rows, :], weight[2 * source], preferred_element_type=jnp.float32
            ) + jnp.dot(
                held[slot, 1, rows, :], weight[2 * source + 1], preferred_element_type=jnp.float32
            )
        return carry

    gather_phases(copy, lambda low, high: lax.fori_loop(low, high, one_slot, 0))
    out_ref[...] = (cols_ref[...].astype(jnp.float32) + scale_ref[...] * total[...]).astype(
        jnp.bfloat16
    )


def mix(qkv_rows, seg_row, input_cols, layer_scale, w_out):
    seq_len, head_width = input_cols.shape
    vmem = pl.BlockSpec(memory_space=pltpu.VMEM)
    return pl.pallas_call(
        mix_body,
        out_shape=jax.ShapeDtypeStruct((seq_len, head_width), jnp.bfloat16),
        in_specs=[vmem] * 5 + [pl.BlockSpec(memory_space=pl.ANY)],
        out_specs=vmem,
        scratch_shapes=[
            pltpu.VMEM((8, 2, seq_len, 2 * HEAD_DIM), jnp.bfloat16),
            pltpu.VMEM((seq_len, head_width), jnp.float32),
            pltpu.VMEM((16, 2 * HEAD_DIM, head_width), jnp.bfloat16),
            pltpu.SemaphoreType.DMA((8, 2)),
            pltpu.SemaphoreType.DMA((8, 2)),
            pltpu.SemaphoreType.DMA,
        ],
        compiler_params=pltpu.CompilerParams(
            collective_id=1, has_side_effects=True, vmem_limit_bytes=56 * 1024 * 1024
        ),
    )(
        qkv_rows,
        seg_row[:, None],
        seg_row[None, :],
        input_cols,
        layer_scale[None, :],
        w_out.reshape(16, 2 * HEAD_DIM, head_width),
    )


def merge_body(rows_ref, w_hbm, out_ref, part, first_in, second_in, third_in, weight,
               send_sem, recv_sem, load_sem):
    me = lax.axis_index("tensor")
    chunks, chunk = weight.shape[0], weight.shape[3]
    loads = [
        pltpu.make_async_copy(
            w_hbm.at[:, :, n * chunk : (n + 1) * chunk], weight.at[n], load_sem.at[n]
        )
        for n in range(chunks)
    ]
    for load in loads:
        load.start()
    greet(me)
    group = part.shape[2]

    def copy(n, index):
        bits = (2, 4) if n % 2 == 0 else (4, 2)
        if index == 0:
            bit, source, target = 1, part.at[n, 0:4], first_in.at[n]
        elif index < 3:
            place = ((5, 7) if bits[0] == 2 else (6, 7))[index - 1]
            bit, source, target = bits[0], part.at[n, place], second_in.at[n, index - 1]
        else:
            bit, source, target = bits[1], part.at[n, 6 if bits[1] == 4 else 5], third_in.at[n]
        peer = me + bit - 2 * bit * lax.rem(lax.div(me, bit), 2)
        return pltpu.make_async_remote_copy(
            src_ref=source,
            dst_ref=target,
            send_sem=send_sem.at[n, index],
            recv_sem=recv_sem.at[n, index],
            device_id={"tensor": peer},
            device_id_type=MESH,
        )

    def add(n, place, arrived):
        total = part[n, place].astype(jnp.float32) + arrived.astype(jnp.float32)
        part[n, place] = total.astype(jnp.bfloat16)

    for step in range(chunks + 3):
        if step < chunks:
            loads[step].wait()
            for place in range(0, 8, 4):
                rows = slice(place * group, (place + 4) * group)
                product = jnp.zeros((4 * group, chunk), jnp.float32)
                for patch in range(4):
                    depth = weight.shape[2]
                    product += jnp.dot(
                        rows_ref[rows, patch * depth : (patch + 1) * depth],
                        weight[step, patch],
                        preferred_element_type=jnp.float32,
                    )
                part[step, place : place + 4] = product.astype(jnp.bfloat16).reshape(
                    4, group, chunk
                )
                if place == 0:
                    copy(step, 0).start()
        n = step - 1
        if 0 <= n < chunks:
            copy(n, 0).wait_recv()
            for place in range(4):
                add(n, 4 + place, first_in[n, place])
            copy(n, 1).start()
            copy(n, 2).start()
        n = step - 2
        if 0 <= n < chunks:
            copy(n, 1).wait_recv()
            copy(n, 2).wait_recv()
            add(n, 4, second_in[n, 0])
            add(n, 6 if n % 2 == 0 else 5, second_in[n, 1])
            copy(n, 3).start()
        n = step - 3
        if 0 <= n < chunks:
            copy(n, 3).wait_recv()
            total = part[n, 4].astype(jnp.float32) + third_in[n].astype(jnp.float32)
            out_ref[:, n * chunk : (n + 1) * chunk] = total.astype(jnp.bfloat16)
    for n in range(chunks):
        for index in range(4):
            copy(n, index).wait_send()


def merge_reduce(by_owner, w_merge):
    group = by_owner.shape[0] // 8
    patches, depth, out_width = w_merge.shape
    chunk = min(512, out_width)
    chunks = out_width // chunk
    vmem = pl.BlockSpec(memory_space=pltpu.VMEM)
    return pl.pallas_call(
        merge_body,
        out_shape=jax.ShapeDtypeStruct((group, out_width), jnp.bfloat16),
        in_specs=[vmem, pl.BlockSpec(memory_space=pl.ANY)],
        out_specs=vmem,
        scratch_shapes=[
            pltpu.VMEM((chunks, 8, group, chunk), jnp.bfloat16),
            pltpu.VMEM((chunks, 4, group, chunk), jnp.bfloat16),
            pltpu.VMEM((chunks, 2, group, chunk), jnp.bfloat16),
            pltpu.VMEM((chunks, group, chunk), jnp.bfloat16),
            pltpu.VMEM((chunks, patches, depth, chunk), jnp.bfloat16),
            pltpu.SemaphoreType.DMA((chunks, 4)),
            pltpu.SemaphoreType.DMA((chunks, 4)),
            pltpu.SemaphoreType.DMA((chunks,)),
        ],
        compiler_params=pltpu.CompilerParams(
            collective_id=2, has_side_effects=True, vmem_limit_bytes=56 * 1024 * 1024
        ),
    )(by_owner, w_merge)


def general_hidden(
    tokens, ln_gain, ln_bias, cos_table, sin_table, w_qkv, seg_row, layer_scale, w_out
):
    model_width = tokens.shape[2]
    col_width = layer_scale.shape[0]
    head_width = w_qkv.shape[2]
    local_heads = head_width // HEAD_DIM
    qkv_weight = jnp.transpose(w_qkv, (1, 0, 2))
    all_tokens = lax.all_gather(tokens[0], "tensor", axis=0, tiled=True)
    normed = layer_norm(all_tokens, ln_gain, ln_bias)
    input_cols = lax.dynamic_slice_in_dim(
        all_tokens, lax.axis_index("tensor") * col_width, col_width, 1
    )
    count_rows = normed.shape[0]
    product = jnp.concatenate(
        [jnp.dot(normed, qkv_weight[n], preferred_element_type=jnp.float32) for n in range(3)], axis=1
    )
    cos_rows = cos_table[:, None, :]
    sin_rows = sin_table[:, None, :]
    query_part = rotate(
        product[:, :head_width].reshape(count_rows, local_heads, HEAD_DIM), cos_rows, sin_rows
    ).reshape(count_rows, head_width)
    key_part = rotate(
        product[:, head_width : 2 * head_width].reshape(count_rows, local_heads, HEAD_DIM),
        cos_rows,
        sin_rows,
    ).reshape(count_rows, head_width)
    qkv_rows = jnp.concatenate([query_part, key_part, product[:, 2 * head_width :]], axis=1).astype(
        jnp.bfloat16
    )[None][0]
    context = attention(qkv_rows, seg_row, local_heads)
    mixed = jnp.dot(
        lax.all_gather(context, "tensor", axis=1, tiled=True),
        w_out,
        preferred_element_type=jnp.float32,
    )
    hidden = (input_cols.astype(jnp.float32) + layer_scale * mixed).astype(jnp.bfloat16)
    return hidden


def local(
    tokens, ln_gain, ln_bias, w_qkv, w_out, layer_scale, w_merge, segment_ids, grid_sizes, owners
):
    tensor_count = lax.axis_size("tensor")
    batch_count = lax.axis_size("dp")
    seg_row = segment_ids[0]
    grid_row = grid_sizes[0]
    owner_row = owners[0, :, 0]
    seq_len = seg_row.shape[0]
    model_width = tokens.shape[2]
    col_width = layer_scale.shape[0]
    head_width = w_qkv.shape[2]
    local_heads = head_width // HEAD_DIM
    merged_rows = seq_len // 4
    device_count = batch_count * tensor_count
    own_cap = max(2, 3 * merged_rows // (2 * device_count))
    out_width = w_merge.shape[2]
    cos_table, sin_table = rope_tables(seg_row, grid_row, seq_len)
    if tensor_count == 8 and head_width == 4 * HEAD_DIM and col_width == head_width:
        qkv_rows, input_cols = project(tokens[0], ln_gain, ln_bias, cos_table, sin_table, w_qkv)
        hidden = mix(qkv_rows, seg_row, input_cols, layer_scale, w_out)
    else:
        hidden = general_hidden(
            tokens, ln_gain, ln_bias, cos_table, sin_table, w_qkv, seg_row, layer_scale, w_out
        )
    sources, is_valid = merge_sources(grid_row, merged_rows)
    merge_weight = w_merge.reshape(4 * col_width, out_width)
    ranks = owner_ranks(owner_row)
    block_rows = batch_count * own_cap
    in_kernel = tensor_count == 8
    group = -(-block_rows // 16) * 16 if in_kernel else block_rows
    owner_place = owner_row % tensor_count
    if in_kernel:
        relative = jnp.bitwise_xor(owner_place, lax.axis_index("tensor"))
        owner_place = relative // 2 + 4 * (1 - relative % 2)
    slot_keys = owner_place * group + (owner_row // tensor_count) * own_cap + ranks
    slot_ids = jnp.arange(tensor_count * group, dtype=jnp.int32)
    placing = (slot_ids[:, None] == slot_keys[None, :]) & is_valid[None, :]
    positions = jnp.arange(seq_len, dtype=jnp.int32)
    picked = []
    for patch in range(4):
        source = jnp.sum(jnp.where(placing, sources[:, patch][None, :] + 1, 0), axis=1) - 1
        onehot = (source[:, None] == positions[None, :]).astype(jnp.bfloat16)
        picked.append(
            jnp.dot(onehot, hidden, preferred_element_type=jnp.float32).astype(jnp.bfloat16)
        )
    by_owner = jnp.concatenate(picked, axis=1)
    if in_kernel:
        owned = merge_reduce(by_owner, w_merge)[:block_rows]
    else:
        group_part = jnp.dot(by_owner, merge_weight, preferred_element_type=jnp.float32).astype(
            jnp.bfloat16
        )
        owned = lax.psum_scatter(group_part, "tensor", scatter_dimension=0, tiled=True)
    arrived = lax.all_to_all(
        owned.reshape(batch_count, own_cap, out_width), "dp", split_axis=0, concat_axis=0, tiled=True
    )
    return arrived.reshape(1, batch_count * own_cap, out_width)


def solution(mesh):
    in_specs = (
        P("dp", "tensor", None),
        P(),
        P(),
        P(None, None, "tensor"),
        P(None, "tensor"),
        P("tensor"),
        P(None, "tensor", None),
        P("dp", None),
        P("dp", None, None),
        P("dp", None, None),
    )
    out_specs = P("dp", "tensor", None)
    return jax.shard_map(local, mesh=mesh, in_specs=in_specs, out_specs=out_specs, check_vma=False)
```
